128 devices in a mesh: wide: 32 (over y, x_hi, z), narrow: 4 (over x_lo, core).
Axes of the slice: x: 4 (x_hi: 2, x_lo: 2; x = x_hi * 2 + x_lo), y: 4, z: 4, core: 2. Of those that a mesh axis runs over, the one named last changes fastest.
Arguments:
- tokens: bfloat16 [1024, 8192], P('wide', 'narrow'), may hold values from -6 to 6
- gate_weight: bfloat16 [8192, 28672], P('narrow', 'wide'), may hold values from -6 to 6
- up_weight: bfloat16 [8192, 28672], P('narrow', 'wide'), may hold values from -6 to 6
- down_weight: bfloat16 [28672, 8192], P('wide', 'narrow'), may hold values from -6 to 6
- gate_left: bfloat16 [256, 8192], P('wide', 'narrow'), may hold values from -6 to 6
- gate_right: bfloat16 [256, 28672], P(None, 'wide'), may hold values from -6 to 6
- up_left: bfloat16 [256, 8192], P('wide', 'narrow'), may hold values from -6 to 6
- up_right: bfloat16 [256, 28672], P(None, 'wide'), may hold values from -6 to 6
- down_left: bfloat16 [256, 28672], P(None, 'wide'), may hold values from -6 to 6
- down_right: bfloat16 [256, 8192], P('wide', 'narrow'), may hold values from -6 to 6
- fitness: float32 [256], replicated, may hold values from -4 to 4
Outputs:
- mlp_out: bfloat16 [1024, 8192], P('wide', 'narrow')
- new_gate: bfloat16 [8192, 28672], P('narrow', 'wide')
- new_up: bfloat16 [8192, 28672], P('narrow', 'wide')
- new_down: bfloat16 [28672, 8192], P('wide', 'narrow')
The draws below stay inside these ranges and needn't reach their ends.
All inputs are finite; a program needn't handle non-finite values.
Results may differ from the reference program's by a relative error of at most 0.0049.
Values may be sent and summed in bfloat16 or wider, within the bound.
No kernel may reach another device: no remote copies, remote signals or barrier semaphores. Data moves between devices by JAX's collectives and lax.ppermute only.
A program may use at most 128 MiB of HBM per device.

```python
import math
import jax
import jax.numpy as jnp

D = 8192
FF = 28672
TPM = 4
MEMBERS = 256
ROWS = 1024


def level_of(own_key, shape, shards, least, top_value):
    def one(axis_at, blocks):
        heights = jax.random.uniform(jax.random.fold_in(jax.random.fold_in(own_key, 6), axis_at), (blocks,), jnp.float32, least / len(shards), top_value / len(shards))
        return jnp.repeat(jnp.exp(heights), shape[axis_at] // blocks).reshape((-1,) + (1,) * (len(shape) - axis_at - 1))

    gain = one(*shards[0])
    for cut in shards[1:]:
        gain = gain * one(*cut)
    return gain


def scatter_about(stream_key, extent, width, bound, shards=(), dtype=jnp.bfloat16):
    level = level_of(stream_key, extent, shards, -0.22, 0.18) if shards else 1.0
    entries = jax.random.normal(stream_key, extent, jnp.float32) * width * level
    return jnp.minimum(jnp.maximum(entries, -bound), bound).astype(dtype)


def setup_inputs(seed: int = 0) -> dict:
    splits = jax.random.split(jax.random.key(seed), 12)
    return {
        "tokens": scatter_about(splits[0], (ROWS, D), 1.0, 6.0, ((0, 32), (1, 4))),
        "gate_weight": scatter_about(splits[1], (D, FF), 1.0, 6.0, ((0, 4), (1, 32))),
        "up_weight": scatter_about(splits[2], (D, FF), 1.0, 6.0, ((0, 4), (1, 32))),
        "down_weight": scatter_about(splits[3], (FF, D), 1.0, 6.0, ((0, 32), (1, 4))),
        "gate_left": scatter_about(splits[4], (MEMBERS, D), 1.0, 6.0, ((0, 32), (1, 4))),
        "gate_right": scatter_about(splits[5], (MEMBERS, FF), 1.0, 6.0, ((1, 32),)),
        "up_left": scatter_about(splits[6], (MEMBERS, D), 1.0, 6.0, ((0, 32), (1, 4))),
        "up_right": scatter_about(splits[7], (MEMBERS, FF), 1.0, 6.0, ((1, 32),)),
        "down_left": scatter_about(splits[8], (MEMBERS, FF), 1.0, 6.0, ((1, 32),)),
        "down_right": scatter_about(splits[9], (MEMBERS, D), 1.0, 6.0, ((0, 32), (1, 4))),
        "fitness": scatter_about(splits[10], (MEMBERS,), 1.0, 4.0, (), jnp.float32),
    }


noise_scale = 0.5
step_size = 0.5

def perturbed(inputs, weight, projection, right_factor):
    product = jnp.dot(inputs, weight, preferred_element_type=jnp.float32)
    shaped = product.reshape(MEMBERS, TPM, product.shape[1])
    shaped = shaped + noise_scale * projection[:, :, None] * right_factor.astype(jnp.float32)[:, None, :]
    return shaped.reshape(product.shape)

def member_dots(inputs, left_factor):
    grouped = inputs.astype(jnp.float32).reshape(MEMBERS, TPM, inputs.shape[1])
    return jnp.einsum('mtk,mk->mt', grouped, left_factor.astype(jnp.float32))

def apply_update(weight, left_factor, right_factor):
    update_term = jnp.dot(left_factor.T, right_factor, preferred_element_type=jnp.float32)
    step_coef = step_size / math.sqrt(MEMBERS)
    return (weight.astype(jnp.float32) + step_coef * update_term).astype(jnp.bfloat16)

def reference(tokens, gate_weight, up_weight, down_weight, gate_left, gate_right, up_left, up_right, down_left, down_right, fitness):
    gate_proj = member_dots(tokens, gate_left)
    up_proj = member_dots(tokens, up_left)
    gate = perturbed(tokens, gate_weight, gate_proj, gate_right) * D ** (-0.5)
    up = perturbed(tokens, up_weight, up_proj, up_right) * D ** (-0.5)
    hidden = (jax.nn.silu(gate) * up).astype(jnp.bfloat16)
    down_proj = member_dots(hidden, down_left)
    mlp_out = (perturbed(hidden, down_weight, down_proj, down_right) * FF ** (-0.5)).astype(jnp.bfloat16)
    weights_col = fitness.astype(jnp.float32)[:, None]
    weighted_gate = (gate_left.astype(jnp.float32) * weights_col).astype(jnp.bfloat16)
    weighted_up = (up_left.astype(jnp.float32) * weights_col).astype(jnp.bfloat16)
    weighted_down = (down_right.astype(jnp.float32) * weights_col).astype(jnp.bfloat16)
    new_gate = apply_update(gate_weight, weighted_gate, gate_right)
    new_up = apply_update(up_weight, weighted_up, up_right)
    new_down = apply_update(down_weight, down_left, weighted_down)
    return (mlp_out, new_gate, new_up, new_down)
```

```python
import math

import jax
import jax.numpy as jnp
from jax import lax
from jax.experimental import pallas as pl
from jax.experimental.pallas import tpu as pltpu
from jax.sharding import PartitionSpec as P

NY, NH, NZ = 4, 2, 4
STEPS = (0, 1, 3, 2)
LANES = 128
noise_scale = 0.5
step_size = 0.5

f32, bf16 = jnp.float32, jnp.bfloat16
SCOPED = 12 << 20
COST = pl.CostEstimate(flops=1000, bytes_accessed=1000, transcendentals=0)


def wide_index(y, h, z):
    return (y % NY) * (NH * NZ) + (h % NH) * NZ + z % NZ


def wide_perm(dy, dh, dz):
    return [
        (wide_index(y + dy, h + dh, z + dz), wide_index(y, h, z))
        for y in range(NY)
        for h in range(NH)
        for z in range(NZ)
    ]


def by_core(first, second):
    return [
        (4 * i + n, 4 * j + n)
        for n in range(4)
        for i, j in (second if n % 2 else first)
    ]


def early(x, d, name):
    pairs = by_core(wide_perm(0, 0, d), wide_perm(d, 0, 0))
    with jax.named_scope(name):
        return lax.ppermute(x, ("wide", "narrow"), pairs)


def late(x, d, name):
    pairs = by_core(wide_perm(d, 0, 0), wide_perm(0, 0, d))
    with jax.named_scope(name):
        return lax.ppermute(x, ("wide", "narrow"), pairs)


def from_h(x, name):
    with jax.named_scope(name):
        return lax.ppermute(x, "wide", wide_perm(0, 1, 0))


def from_core(pieces, name):
    with jax.named_scope(name):
        pairs = [(n, n ^ 1) for n in range(4)]
        return [lax.ppermute(p, "narrow", pairs) for p in pieces]


def from_x(x, name):
    with jax.named_scope(name):
        return lax.ppermute(x, "narrow", [(n, n ^ 2) for n in range(4)])


def after(x, *others):
    return lax.optimization_barrier((x, *others))[0]


VMEM = pl.BlockSpec(memory_space=pltpu.VMEM)
SMEM = pl.BlockSpec(memory_space=pltpu.SMEM)
ANY = pl.BlockSpec(memory_space=pl.ANY)


def call(kernel, outs, in_specs, name, scratch=(), out_specs=None):
    if out_specs is None:
        out_specs = tuple(VMEM for _ in outs)
        out_shape = tuple(pltpu.VMEM(s, t) for s, t in outs)
    else:
        out_shape = tuple(jax.ShapeDtypeStruct(s, t) for s, t in outs)
    return pl.pallas_call(
        kernel,
        out_shape=out_shape,
        in_specs=in_specs,
        out_specs=out_specs,
        scratch_shapes=list(scratch),
        compiler_params=pltpu.CompilerParams(vmem_limit_bytes=SCOPED),
        cost_estimate=COST,
        name=name,
    )


def in_hbm(x):
    return pltpu.with_memory_space_constraint(x, pltpu.HBM)


def steps_of(r):
    return r ^ (r >> 1)


def one_hot(m, members):
    return (m == lax.broadcasted_iota(jnp.int32, m.shape, 1)).astype(bf16)


def members_of(where, d, part, rows, half, own, per, members):
    r = lax.broadcasted_iota(jnp.int32, (rows, members), 0)
    s = steps_of(r // (NH * half))
    y = where[1] + jnp.where(part == 0, d, s)
    z = where[3] + jnp.where(part == 0, s, d)
    m = wide_index(y, where[2] + r // half, z) * own + (r % half) // per + part * (own // 2)
    return one_hot(m, members)


def gathered_order(where, own, members):
    r = lax.broadcasted_iota(jnp.int32, (members, members), 0)
    late_step, early_step = steps_of(r // (NZ * NH * own)), steps_of(r // (NH * own) % NZ)
    first = where[0] == 0
    y = where[1] + jnp.where(first, late_step, early_step)
    z = where[3] + jnp.where(first, early_step, late_step)
    return one_hot(wide_index(y, where[2] + r // own, z) * own + r % own, members)


def prepare(where, fitness, tokens, gate_left, up_left, down_right):
    rows, deep = tokens.shape
    own = gate_left.shape[0]
    arrays = (tokens, gate_left, up_left, down_right)

    def kernel(where, fitness, *refs):
        sources, (packed, weighted), (tok, gl, ul, dr, sem) = refs[:4], refs[4:6], refs[6:]
        copies = [
            pltpu.make_async_copy(a, b, sem.at[i])
            for i, (a, b) in enumerate(zip(sources, (tok, gl, ul, dr)))
        ]
        for c in copies:
            c.start()
        for c in copies:
            c.wait()
        packed[:, :deep] = tok[...]
        r = lax.broadcasted_iota(jnp.int32, (rows, own), 0)
        whose = r // (rows // own) == lax.broadcasted_iota(jnp.int32, (rows, own), 1)
        lane = lax.broadcasted_iota(jnp.int32, (rows, LANES), 1)
        extra = jnp.zeros((rows, LANES), f32)
        for c, left in enumerate((gl, ul)):
            dots = lax.dot_general(
                tok[...], left[...], (((1,), (1,)), ((), ())), preferred_element_type=f32
            )
            proj = jnp.sum(jnp.where(whose, dots, 0.0), 1, keepdims=True)
            high = proj.astype(bf16).astype(f32)
            extra = jnp.where(lane == 2 * c, high, extra)
            extra = jnp.where(lane == 2 * c + 1, proj - high, extra)
        packed[:, deep:] = extra.astype(bf16)
        w = (where[1] * NH + where[2]) * NZ + where[3]
        r = lax.broadcasted_iota(jnp.int32, (own, LANES), 0)
        fit = jnp.zeros((own, LANES), f32)
        for i in range(own):
            fit = jnp.where(r == i, fitness[w * own + i], fit)
        for c, left in enumerate((gl, ul, dr)):
            weighted[:, c * deep : (c + 1) * deep] = (
                left[...].astype(f32) * fit[:, :1]
            ).astype(bf16)

    return call(
        kernel,
        [((rows, deep + LANES), bf16), ((own, 3 * deep), bf16)],
        [SMEM, SMEM] + [ANY] * 4,
        "prepare",
        [pltpu.VMEM(v.shape, v.dtype) for v in arrays] + [pltpu.SemaphoreType.DMA((4,))],
    )(where, fitness, *[in_hbm(v) for v in arrays])


def resident(*arrays):
    n, parts = len(arrays), 4

    def kernel(*refs):
        src, dst, sem = refs[:n], refs[n : 2 * n], refs[2 * n]
        copies = []
        for i in range(n):
            step = src[i].shape[0] // parts
            for q in range(parts):
                rows = pl.ds(q * step, step)
                copies.append(
                    pltpu.make_async_copy(src[i].at[rows], dst[i].at[rows], sem.at[i, q])
                )
        for c in copies:
            c.start()
        for c in copies:
            c.wait()

    return call(
        kernel,
        [(v.shape, v.dtype) for v in arrays],
        [ANY] * n,
        "resident",
        [pltpu.SemaphoreType.DMA((n, parts))],
    )(*[in_hbm(v) for v in arrays])


def split_halves(where, own, over):
    rows, cols = own.shape
    half = rows // 2

    def kernel(where, own, over, mine, theirs):
        a = jnp.concatenate([own[:half, :], over[:half, :]], 0)
        b = jnp.concatenate([own[half:, :], over[half:, :]], 0)
        first = where[0] == 0
        mine[...] = jnp.where(first, a, b)
        theirs[...] = jnp.where(first, b, a)

    return call(kernel, [((rows, cols), own.dtype)] * 2, [SMEM, VMEM, VMEM], "split_halves")(
        where, own, over
    )


def stack(parts, pieces=1):
    cols, n = parts[0].shape[1], len(parts)

    def kernel(*refs):
        at = 0
        for q in range(pieces):
            for ref in refs[:n]:
                step = ref.shape[0] // pieces
                refs[n][at : at + step, :] = ref[q * step : (q + 1) * step, :]
                at += step

    rows = sum(p.shape[0] for p in parts)
    return call(kernel, [((rows, cols), parts[0].dtype)], [VMEM] * n, "stack")(*parts)[0]


def cut(x, start, count):
    rows, cols = x.shape
    step = (rows - start) // count

    def kernel(x, *outs):
        for i, out in enumerate(outs):
            out[...] = x[start + i * step : start + (i + 1) * step, :]

    return call(kernel, [((step, cols), x.dtype)] * count, [VMEM], "cut")(x)


def whole(refs):
    return jnp.concatenate([r[...] for r in refs], 0)


def gate_up(where, d, own, per, x, others, wg, wu, rg, ru):
    rows, deep, n = x.shape[0] // 2, wg.shape[0], len(others)
    cols, members = wg.shape[1], rg.shape[0]
    tile, step = 2 * LANES, rows // n

    def kernel(where, x, *refs):
        xo, (wg, wu, rg, ru, keep), send = refs[:n], refs[n : n + 5], refs[n + 5 :]
        xs = jnp.concatenate([x[:rows, :deep]] + [r[:, :deep] for r in xo], 0)
        proj = jnp.concatenate([x[:rows, deep:]] + [r[:, deep:] for r in xo], 0).astype(f32)
        pick = jnp.concatenate(
            [
                members_of(where, d, part, rows, own * per // 2, own, per, members)
                for part in (where[0], 1 - where[0])
            ],
            0,
        )
        for j, (w, r) in enumerate(((wg, rg), (wu, ru))):
            scale = noise_scale * (proj[:, 2 * j : 2 * j + 1] + proj[:, 2 * j + 1 : 2 * j + 2])
            for t in range(0, cols, tile):
                at = slice(t, min(cols, t + tile))
                prod = jnp.dot(xs, w[:, at], preferred_element_type=f32)
                prod += scale * jnp.dot(pick, r[:, at], preferred_element_type=f32)
                to = slice(j * cols + at.start, j * cols + at.stop)
                keep[:, to] = prod[:rows]
                for i, out in enumerate(send):
                    out[:, to] = prod[rows + i * step : rows + (i + 1) * step]

    keep, *send = call(
        kernel,
        [((rows, 2 * cols), f32)] + [((step, 2 * cols), f32)] * n,
        [SMEM] + [VMEM] * (n + 5),
        f"gate_up{d}",
    )(where, x, *others, wg, wu, rg, ru)
    return keep, send


def add_both(kept, pieces, name):
    n, cols = len(kept), kept[0].shape[1]
    rows = sum(a.shape[0] for a in kept)

    def kernel(*refs):
        total, coarse = refs[-2:]
        s = whole(refs[:n]) + whole(refs[n:-2])
        total[...] = s
        coarse[...] = s.astype(bf16)

    return call(
        kernel, [((rows, cols), f32), ((rows, cols), bf16)], [VMEM] * (n + len(pieces)), name
    )(*kept, *pieces)


def hidden_units(mine, other, scale, pieces, name):
    rows, cols = mine.shape
    n, step = cols // 2, rows // pieces

    def kernel(mine, other, *outs):
        gate = (mine[:, :n] + other[:, :n].astype(f32)) * scale
        up = (mine[:, n:] + other[:, n:].astype(f32)) * scale
        hidden = (jax.nn.silu(gate) * up).astype(bf16)
        for i, out in enumerate(outs):
            out[...] = hidden[i * step : (i + 1) * step]

    return list(call(kernel, [((step, n), bf16)] * pieces, [VMEM, VMEM], name)(mine, other))


def down(where, steps, own, per, mine, others, wd, left, dtype, pieces, name):
    n, rows = len(mine), sum(m.shape[0] for m in mine)
    cols = wd.shape[1]
    each, count = rows // len(steps), pieces * len(steps)
    tile, step = 4 * LANES, rows // count

    def kernel(where, *refs):
        hm, ho, (wd, left), outs = refs[:n], refs[n : 2 * n], refs[2 * n : 2 * n + 2], refs[2 * n + 2 :]
        both = jnp.concatenate([whole(hm), whole(ho)], 0)
        pick = jnp.concatenate(
            [
                members_of(where, d, part, each, own * per // 2, own, per, left.shape[0])
                for part in (where[0], 1 - where[0])
                for d in steps
            ],
            0,
        )
        rows_left = jnp.dot(pick, left[...], preferred_element_type=f32)
        proj = jnp.sum(both.astype(f32) * rows_left, axis=1, keepdims=True)
        proj = jnp.broadcast_to(proj, (2 * rows, LANES))
        for t in range(0, cols + LANES, tile):
            at = slice(t, min(cols, t + tile)) if t < cols else slice(cols, cols + LANES)
            prod = jnp.dot(both, wd[:, at], preferred_element_type=f32) if t < cols else proj
            for i, out in enumerate(outs):
                out[:, at] = prod[i * step : (i + 1) * step].astype(dtype)

    outs = call(
        kernel,
        [((step, cols + LANES), dtype)] * (2 * count),
        [SMEM] + [VMEM] * (2 * n + 2),
        name,
    )(where, *mine, *others, wd, left)
    return list(outs[:count]), list(outs[count:])


def fold(base, got, pieces):
    rows, cols = got[0].shape
    half, step = rows // 2, rows // 2 // pieces
    n = len(base)

    def kernel(*refs):
        base_refs, got_refs, outs = refs[:n], refs[n : n + len(got)], refs[n + len(got) :]
        each = rows // n
        for c in range(pieces):
            for q in range(2):
                at = q * half + c * step
                b = base_refs[at // each]
                s = b[at % each : at % each + step, :].astype(f32)
                for g in got_refs:
                    s += g[at : at + step, :].astype(f32)
                outs[c][q * step : (q + 1) * step, :] = s.astype(outs[c].dtype)

    return call(
        kernel,
        [((2 * step, cols), bf16 if c else f32) for c in range(pieces)],
        [VMEM] * (n + len(got)),
        "fold",
    )(*base, *got)


def finish(where, mine, theirs, down_right, scale):
    half, deep = mine.shape[0], down_right.shape[1]
    rows, own = 2 * half, down_right.shape[0]

    def kernel(where, mine, theirs, right, out):
        first = where[0] == 0
        a = jnp.where(first, mine[...], theirs[...])
        b = jnp.where(first, theirs[...], mine[...])
        total = jnp.concatenate([a, b], 0)
        r = lax.broadcasted_iota(jnp.int32, (rows, own), 0) // (rows // own)
        pick = (r == lax.broadcasted_iota(jnp.int32, (rows, own), 1)).astype(bf16)
        right_rows = jnp.dot(pick, right[...], preferred_element_type=f32)
        shaped = total[:, :deep] + noise_scale * total[:, deep : deep + 1] * right_rows
        out[...] = (shaped * scale).astype(out.dtype)

    return call(
        kernel,
        [((rows, deep), bf16)],
        [SMEM] + [VMEM] * 3,
        "finish",
        out_specs=(VMEM,),
    )(where, mine, theirs, down_right)[0]


def update(where, own, factors, start, right, weight, step_coef, transposed=False):
    rows, cols = weight.shape
    members, n = right.shape[0], len(factors)
    parts = 4 if rows % (4 * LANES) == 0 else max(1, rows // LANES)
    step = rows // parts

    def kernel(where, *refs):
        pieces, (r, w, out, buf, sem) = refs[:n], refs[n:]
        order = gathered_order(where, own, members)
        moved = jnp.dot(order, r[...], preferred_element_type=f32).astype(bf16)
        copies = []
        for i in range(parts):
            at = slice(i * step, (i + 1) * step)
            take = slice(start, start + cols) if transposed else slice(start + i * step, start + (i + 1) * step)
            side = jnp.concatenate([p[:, take] for p in pieces], 0)
            left, other = (moved[:, at], side) if transposed else (side, moved)
            term = lax.dot_general(
                left, other, (((0,), (0,)), ((), ())), preferred_element_type=f32
            )
            buf[at, :] = (w[at, :].astype(f32) + step_coef * term).astype(bf16)
            here = pl.ds(i * step, step)
            copies.append(pltpu.make_async_copy(buf.at[here], out.at[here], sem.at[i]))
            copies[-1].start()
        for c in copies:
            c.wait()

    return call(
        kernel,
        [((rows, cols), weight.dtype)],
        [SMEM] + [VMEM] * (n + 2),
        "update",
        [pltpu.VMEM((rows, cols), bf16), pltpu.SemaphoreType.DMA((parts,))],
        out_specs=(ANY,),
    )(where, *factors, right, weight)[0]


def on_device(
    tokens,
    gate_weight,
    up_weight,
    down_weight,
    gate_left,
    gate_right,
    up_left,
    up_right,
    down_left,
    down_right,
    fitness,
):
    rows, deep = tokens.shape
    own = gate_left.shape[0]
    members = fitness.shape[0]
    per = rows // own
    d_model = deep * lax.axis_size("narrow")
    d_hidden = gate_weight.shape[1] * lax.axis_size("wide")
    w = lax.axis_index("wide")
    where = jnp.stack(
        [lax.axis_index("narrow") % 2, w // (NH * NZ), (w // NZ) % NH, w % NZ]
    ).astype(jnp.int32)

    packed, weighted = prepare(where, fitness, tokens, gate_left, up_left, down_right)

    over = from_h(packed, "tokens_xhi")
    weighted_over = from_h(weighted, "factors_xhi")
    gate_weight, up_weight = resident(after(gate_weight, packed), up_weight)
    mine, theirs = split_halves(where, after(packed, gate_weight, weighted_over), over)
    block = stack([mine] + from_core([theirs], "tokens_core"))
    parts = [block] + [early(block, d, f"tokens_early{d}") for d in STEPS[1:]]
    (down_weight,) = resident(after(down_weight, block))
    line = stack([after(block, down_weight)] + parts[1:], 2)
    lines = {0: line, **{d: late(line, d, f"tokens_late{d}") for d in STEPS[1:3]}}
    lines[2] = late(after(line, lines[1]), 2, "tokens_late2")
    n = line.shape[0] // 2

    def project(d, x, *before):
        others = after(from_core(cut(x, n, 4), f"rows_core{d}"), *before)
        return gate_up(where, d, own, per, x, others, gate_weight, up_weight, gate_right, up_right)

    def activate(mine, other, pieces, name):
        return hidden_units(mine, other, d_model**-0.5, pieces, name)

    def contract(steps, hidden, others, dtype, pieces, name):
        kept, sent = down(
            where, steps, own, per, hidden, others, down_weight, down_left, dtype, pieces, name
        )
        return kept, from_core(sent, f"{name}_core")

    keep0, send0 = project(0, line)
    mine0, coarse0 = add_both([keep0], from_core(send0, "sums_core0"), "add0")
    other0 = from_x(coarse0, "sums_x0")

    weighted = jnp.concatenate([weighted, weighted_over], 0)
    weighted = after(weighted, keep0)
    factor_line = stack([weighted] + [early(weighted, d, f"factors_early{d}") for d in STEPS[1:]])
    factors = {0: factor_line, **{d: late(factor_line, d, f"factors_late{d}") for d in STEPS[1:]}}

    keep1, send1 = project(1, after(lines[1], coarse0, factor_line))
    got1 = from_core(send1, "sums_core1")
    keep3, send3 = project(3, after(lines[3], keep1), got1)
    got = got1 + after(from_core(send3, "sums_core3"), other0)
    mine13, coarse13 = add_both([keep1, keep3], got, "add13")
    other13 = from_x(coarse13, "sums_x13")

    keep2, send2 = project(2, after(lines[2], coarse13, factors[1], factors[3]))
    mine2, coarse2 = add_both([keep2], from_core(send2, "sums_core2"), "add2")
    other2 = from_x(coarse2, "sums_x2")

    hidden0 = activate(after(mine0, coarse13), other0, 2, "hidden0")
    hidden0_o = from_core(hidden0, "hidden_core0")
    kept0, sent0 = contract([0], after(hidden0, coarse2), hidden0_o, f32, 4, "down0")

    hidden13 = activate(after(mine13, coarse2, kept0, factors[2]), other13, 4, "hidden13")
    hidden13_o = from_core(hidden13, "hidden_core13")
    kept, sent = contract([1, 3], hidden13, hidden13_o, bf16, 2, "down13")
    kept = after(kept, other2)
    out1, out3 = stack(kept[:2] + sent[:2]), stack(kept[2:] + sent[2:])
    sum1, sum3 = late(out1, 3, "out_late1"), late(out3, 1, "out_late3")

    hidden2 = activate(after(mine2, out1, out3), other2, 2, "hidden2")
    kept, sent = contract([2], hidden2, from_core(hidden2, "hidden_core2"), bf16, 4, "down2")
    out2 = stack(kept + sent)
    sum2 = late(out2, 2, "out_late2")

    step_coef = step_size / math.sqrt(members)
    factors = after([factors[d] for d in STEPS], out2)
    new_gate = update(where, own, factors, 0, gate_right, gate_weight, step_coef)
    factors = after(factors, new_gate, sum1, sum3)
    new_up = update(where, own, factors, deep, up_right, up_weight, step_coef)
    new_down = update(
        where, own, factors, 2 * deep, down_left, down_weight, step_coef, True
    )

    got = [after(sum1, new_up, new_down), sum3, sum2]
    pieces = fold(kept0 + sent0, got, len(STEPS))
    got = [early(p, 4 - d, f"out_early{d}") for p, d in zip(pieces[1:], STEPS[1:])]
    ours, away = fold([pieces[0]], got, NH)
    both = fold([ours], [from_h(away, "out_xhi")], 1)[0]
    half = rows // 2
    (theirs,) = from_core([both[half:]], "out_core")
    mlp_out = finish(where, both[:half], theirs, down_right, d_hidden**-0.5)
    return (mlp_out, new_gate, new_up, new_down)


def solution(mesh):
    placed = (
        P("wide", "narrow"),
        P("narrow", "wide"),
        P("narrow", "wide"),
        P("wide", "narrow"),
        P("wide", "narrow"),
        P(None, "wide"),
        P("wide", "narrow"),
        P(None, "wide"),
        P(None, "wide"),
        P("wide", "narrow"),
        P(),
    )
    return jax.shard_map(
        on_device,
        mesh=mesh,
        in_specs=placed,
        out_specs=(
            P("wide", "narrow"),
            P("narrow", "wide"),
            P("narrow", "wide"),
            P("wide", "narrow"),
        ),
        check_vma=False,
    )
```

```python
import math

import jax
import jax.numpy as jnp
from jax import lax
from jax.experimental import pallas as pl
from jax.experimental.pallas import tpu as pltpu
from jax.sharding import PartitionSpec as P

NY, NH, NZ = 4, 2, 4
STEPS = (0, 1, 3, 2)
LANES = 128
noise_scale = 0.5
step_size = 0.5

f32, bf16 = jnp.float32, jnp.bfloat16
SCOPED = 12 << 20
COST = pl.CostEstimate(flops=1000, bytes_accessed=1000, transcendentals=0)


def wide_index(y, h, z):
    return (y % NY) * (NH * NZ) + (h % NH) * NZ + z % NZ


def wide_perm(dy, dh, dz):
    return [
        (wide_index(y + dy, h + dh, z + dz), wide_index(y, h, z))
        for y in range(NY)
        for h in range(NH)
        for z in range(NZ)
    ]


def by_core(first, second):
    return [
        (4 * i + n, 4 * j + n)
        for n in range(4)
        for i, j in (second if n % 2 else first)
    ]


def early(x, d, name):
    pairs = by_core(wide_perm(0, 0, d), wide_perm(d, 0, 0))
    with jax.named_scope(name):
        return lax.ppermute(x, ("wide", "narrow"), pairs)


def late(x, d, name):
    pairs = by_core(wide_perm(d, 0, 0), wide_perm(0, 0, d))
    with jax.named_scope(name):
        return lax.ppermute(x, ("wide", "narrow"), pairs)


def from_h(x, name):
    with jax.named_scope(name):
        return lax.ppermute(x, "wide", wide_perm(0, 1, 0))


def from_core(pieces, name):
    with jax.named_scope(name):
        pairs = [(n, n ^ 1) for n in range(4)]
        return [lax.ppermute(p, "narrow", pairs) for p in pieces]


def from_x(x, name):
    with jax.named_scope(name):
        return lax.ppermute(x, "narrow", [(n, n ^ 2) for n in range(4)])


def after(x, *others):
    return lax.optimization_barrier((x, *others))[0]


VMEM = pl.BlockSpec(memory_space=pltpu.VMEM)
SMEM = pl.BlockSpec(memory_space=pltpu.SMEM)
ANY = pl.BlockSpec(memory_space=pl.ANY)


def call(kernel, outs, in_specs, name, scratch=(), out_specs=None):
    if out_specs is None:
        out_specs = tuple(VMEM for _ in outs)
        out_shape = tuple(pltpu.VMEM(s, t) for s, t in outs)
    else:
        out_shape = tuple(jax.ShapeDtypeStruct(s, t) for s, t in outs)
    return pl.pallas_call(
        kernel,
        out_shape=out_shape,
        in_specs=in_specs,
        out_specs=out_specs,
        scratch_shapes=list(scratch),
        compiler_params=pltpu.CompilerParams(vmem_limit_bytes=SCOPED),
        cost_estimate=COST,
        name=name,
    )


def in_hbm(x):
    return pltpu.with_memory_space_constraint(x, pltpu.HBM)


def steps_of(r):
    return r ^ (r >> 1)


def one_hot(m, members):
    return (m == lax.broadcasted_iota(jnp.int32, m.shape, 1)).astype(bf16)


def members_of(where, d, part, rows, half, own, per, members):
    r = lax.broadcasted_iota(jnp.int32, (rows, members), 0)
    s = steps_of(r // (NH * half))
    y = where[1] + jnp.where(part == 0, d, s)
    z = where[3] + jnp.where(part == 0, s, d)
    m = wide_index(y, where[2] + r // half, z) * own + (r % half) // per + part * (own // 2)
    return one_hot(m, members)


def gathered_order(where, own, members):
    r = lax.broadcasted_iota(jnp.int32, (members, members), 0)
    late_step, early_step = steps_of(r // (NZ * NH * own)), steps_of(r // (NH * own) % NZ)
    first = where[0] == 0
    y = where[1] + jnp.where(first, late_step, early_step)
    z = where[3] + jnp.where(first, early_step, late_step)
    return one_hot(wide_index(y, where[2] + r // own, z) * own + r % own, members)


def prepare(where, fitness, tokens, gate_left, up_left, down_right):
    rows, deep = tokens.shape
    own = gate_left.shape[0]
    arrays = (tokens, gate_left, up_left, down_right, fitness)
    n = len(arrays)

    def kernel(where, *refs):
        sources, (packed, weighted), (*here, sem) = refs[:n], refs[n : n + 2], refs[n + 2 :]
        tok, gl, ul, dr, fitness = here
        copies = [
            pltpu.make_async_copy(a, b, sem.at[i]) for i, (a, b) in enumerate(zip(sources, here))
        ]
        for c in copies:
            c.start()
        for c in copies:
            c.wait()
        packed[:, :deep] = tok[...]
        r = lax.broadcasted_iota(jnp.int32, (rows, own), 0)
        whose = r // (rows // own) == lax.broadcasted_iota(jnp.int32, (rows, own), 1)
        lane = lax.broadcasted_iota(jnp.int32, (rows, LANES), 1)
        extra = jnp.zeros((rows, LANES), f32)
        for c, left in enumerate((gl, ul)):
            dots = lax.dot_general(
                tok[...], left[...], (((1,), (1,)), ((), ())), preferred_element_type=f32
            )
            proj = jnp.sum(jnp.where(whose, dots, 0.0), 1, keepdims=True)
            high = proj.astype(bf16).astype(f32)
            extra = jnp.where(lane == 2 * c, high, extra)
            extra = jnp.where(lane == 2 * c + 1, proj - high, extra)
        packed[:, deep:] = extra.astype(bf16)
        w = (where[1] * NH + where[2]) * NZ + where[3]
        r = lax.broadcasted_iota(jnp.int32, (own, LANES), 0)
        fit = jnp.zeros((own, LANES), f32)
        for i in range(own):
            fit = jnp.where(r == i, fitness[w * own + i], fit)
        for c, left in enumerate((gl, ul, dr)):
            weighted[:, c * deep : (c + 1) * deep] = (
                left[...].astype(f32) * fit[:, :1]
            ).astype(bf16)

    return call(
        kernel,
        [((rows, deep + LANES), bf16), ((own, 3 * deep), bf16)],
        [SMEM] + [ANY] * n,
        "prepare",
        [pltpu.VMEM(v.shape, v.dtype) for v in arrays[:4]]
        + [pltpu.SMEM(fitness.shape, f32), pltpu.SemaphoreType.DMA((n,))],
    )(where, *[in_hbm(v) for v in arrays])


def resident(*arrays):
    n, parts = len(arrays), 4

    def kernel(*refs):
        src, dst, sem = refs[:n], refs[n : 2 * n], refs[2 * n]
        copies = []
        for i in range(n):
            step = src[i].shape[0] // parts
            for q in range(parts):
                rows = pl.ds(q * step, step)
                copies.append(
                    pltpu.make_async_copy(src[i].at[rows], dst[i].at[rows], sem.at[i, q])
                )
        for c in copies:
            c.start()
        for c in copies:
            c.wait()

    return call(
        kernel,
        [(v.shape, v.dtype) for v in arrays],
        [ANY] * n,
        "resident",
        [pltpu.SemaphoreType.DMA((n, parts))],
    )(*[in_hbm(v) for v in arrays])


def split_halves(where, own, over):
    rows, cols = own.shape
    half = rows // 2

    def kernel(where, own, over, mine, theirs):
        a = jnp.concatenate([own[:half, :], over[:half, :]], 0)
        b = jnp.concatenate([own[half:, :], over[half:, :]], 0)
        first = where[0] == 0
        mine[...] = jnp.where(first, a, b)
        theirs[...] = jnp.where(first, b, a)

    return call(kernel, [((rows, cols), own.dtype)] * 2, [SMEM, VMEM, VMEM], "split_halves")(
        where, own, over
    )


def stack(parts, pieces=1):
    cols, n = parts[0].shape[1], len(parts)

    def kernel(*refs):
        at = 0
        for q in range(pieces):
            for ref in refs[:n]:
                step = ref.shape[0] // pieces
                refs[n][at : at + step, :] = ref[q * step : (q + 1) * step, :]
                at += step

    rows = sum(p.shape[0] for p in parts)
    return call(kernel, [((rows, cols), parts[0].dtype)], [VMEM] * n, "stack")(*parts)[0]


def cut(x, start, count):
    rows, cols = x.shape
    step = (rows - start) // count

    def kernel(x, *outs):
        for i, out in enumerate(outs):
            out[...] = x[start + i * step : start + (i + 1) * step, :]

    return call(kernel, [((step, cols), x.dtype)] * count, [VMEM], "cut")(x)


def whole(refs):
    return jnp.concatenate([r[...] for r in refs], 0)


def gate_up(where, d, own, per, x, others, wg, wu, rg, ru):
    rows, deep, n = x.shape[0] // 2, wg.shape[0], len(others)
    cols, members = wg.shape[1], rg.shape[0]
    tile, step = 2 * LANES, rows // n

    def kernel(where, x, *refs):
        xo, (wg, wu, rg, ru, keep), send = refs[:n], refs[n : n + 5], refs[n + 5 :]
        xs = jnp.concatenate([x[:rows, :deep]] + [r[:, :deep] for r in xo], 0)
        proj = jnp.concatenate([x[:rows, deep:]] + [r[:, deep:] for r in xo], 0).astype(f32)
        pick = jnp.concatenate(
            [
                members_of(where, d, part, rows, own * per // 2, own, per, members)
                for part in (where[0], 1 - where[0])
            ],
            0,
        )
        for j, (w, r) in enumerate(((wg, rg), (wu, ru))):
            scale = noise_scale * (proj[:, 2 * j : 2 * j + 1] + proj[:, 2 * j + 1 : 2 * j + 2])
            for t in range(0, cols, tile):
                at = slice(t, min(cols, t + tile))
                prod = jnp.dot(xs, w[:, at], preferred_element_type=f32)
                prod += scale * jnp.dot(pick, r[:, at], preferred_element_type=f32)
                to = slice(j * cols + at.start, j * cols + at.stop)
                keep[:, to] = prod[:rows]
                for i, out in enumerate(send):
                    out[:, to] = prod[rows + i * step : rows + (i + 1) * step]

    keep, *send = call(
        kernel,
        [((rows, 2 * cols), f32)] + [((step, 2 * cols), f32)] * n,
        [SMEM] + [VMEM] * (n + 5),
        f"gate_up{d}",
    )(where, x, *others, wg, wu, rg, ru)
    return keep, send


def add_both(kept, pieces, name):
    n, cols = len(kept), kept[0].shape[1]
    rows = sum(a.shape[0] for a in kept)

    def kernel(*refs):
        total, coarse = refs[-2:]
        s = whole(refs[:n]) + whole(refs[n:-2])
        total[...] = s
        coarse[...] = s.astype(bf16)

    return call(
        kernel, [((rows, cols), f32), ((rows, cols), bf16)], [VMEM] * (n + len(pieces)), name
    )(*kept, *pieces)


def hidden_units(mine, other, scale, pieces, name):
    rows, cols = mine.shape
    n, step = cols // 2, rows // pieces

    def kernel(mine, other, *outs):
        gate = (mine[:, :n] + other[:, :n].astype(f32)) * scale
        up = (mine[:, n:] + other[:, n:].astype(f32)) * scale
        hidden = (jax.nn.silu(gate) * up).astype(bf16)
        for i, out in enumerate(outs):
            out[...] = hidden[i * step : (i + 1) * step]

    return list(call(kernel, [((step, n), bf16)] * pieces, [VMEM, VMEM], name)(mine, other))


def down(where, steps, own, per, mine, others, wd, left, dtype, pieces, name):
    n, rows = len(mine), sum(m.shape[0] for m in mine)
    cols = wd.shape[1]
    each, count = rows // len(steps), pieces * len(steps)
    tile, step = 4 * LANES, rows // count

    def kernel(where, *refs):
        hm, ho, (wd, left), outs = refs[:n], refs[n : 2 * n], refs[2 * n : 2 * n + 2], refs[2 * n + 2 :]
        both = jnp.concatenate([whole(hm), whole(ho)], 0)
        pick = jnp.concatenate(
            [
                members_of(where, d, part, each, own * per // 2, own, per, left.shape[0])
                for part in (where[0], 1 - where[0])
                for d in steps
            ],
            0,
        )
        rows_left = jnp.dot(pick, left[...], preferred_element_type=f32)
        proj = jnp.sum(both.astype(f32) * rows_left, axis=1, keepdims=True)
        proj = jnp.broadcast_to(proj, (2 * rows, LANES))
        for t in range(0, cols + LANES, tile):
            at = slice(t, min(cols, t + tile)) if t < cols else slice(cols, cols + LANES)
            prod = jnp.dot(both, wd[:, at], preferred_element_type=f32) if t < cols else proj
            for i, out in enumerate(outs):
                out[:, at] = prod[i * step : (i + 1) * step].astype(dtype)

    outs = call(
        kernel,
        [((step, cols + LANES), dtype)] * (2 * count),
        [SMEM] + [VMEM] * (2 * n + 2),
        name,
    )(where, *mine, *others, wd, left)
    return list(outs[:count]), list(outs[count:])


def fold(base, got, pieces):
    rows, cols = got[0].shape
    half, step = rows // 2, rows // 2 // pieces
    n = len(base)

    def kernel(*refs):
        base_refs, got_refs, outs = refs[:n], refs[n : n + len(got)], refs[n + len(got) :]
        each = rows // n
        for c in range(pieces):
            for q in range(2):
                at = q * half + c * step
                b = base_refs[at // each]
                s = b[at % each : at % each + step, :].astype(f32)
                for g in got_refs:
                    s += g[at : at + step, :].astype(f32)
                outs[c][q * step : (q + 1) * step, :] = s.astype(outs[c].dtype)

    return call(
        kernel,
        [((2 * step, cols), bf16 if c else f32) for c in range(pieces)],
        [VMEM] * (n + len(got)),
        "fold",
    )(*base, *got)


def finish(where, mine, theirs, down_right, scale):
    half, deep = mine.shape[0], down_right.shape[1]
    rows, own = 2 * half, down_right.shape[0]

    def kernel(where, mine, theirs, right, out):
        first = where[0] == 0
        a = jnp.where(first, mine[...], theirs[...])
        b = jnp.where(first, theirs[...], mine[...])
        total = jnp.concatenate([a, b], 0)
        r = lax.broadcasted_iota(jnp.int32, (rows, own), 0) // (rows // own)
        pick = (r == lax.broadcasted_iota(jnp.int32, (rows, own), 1)).astype(bf16)
        right_rows = jnp.dot(pick, right[...], preferred_element_type=f32)
        shaped = total[:, :deep] + noise_scale * total[:, deep : deep + 1] * right_rows
        out[...] = (shaped * scale).astype(out.dtype)

    return call(
        kernel,
        [((rows, deep), bf16)],
        [SMEM] + [VMEM] * 3,
        "finish",
        out_specs=(VMEM,),
    )(where, mine, theirs, down_right)[0]


def update(where, own, factors, start, right, weight, step_coef, transposed=False):
    rows, cols = weight.shape
    members, n = right.shape[0], len(factors)
    parts = 4 if rows % (4 * LANES) == 0 else max(1, rows // LANES)
    step = rows // parts

    def kernel(where, *refs):
        pieces, (r, w, out, buf, sem) = refs[:n], refs[n:]
        order = gathered_order(where, own, members)
        moved = jnp.dot(order, r[...], preferred_element_type=f32).astype(bf16)
        copies = []
        for i in range(parts):
            at = slice(i * step, (i + 1) * step)
            take = slice(start, start + cols) if transposed else slice(start + i * step, start + (i + 1) * step)
            side = jnp.concatenate([p[:, take] for p in pieces], 0)
            left, other = (moved[:, at], side) if transposed else (side, moved)
            term = lax.dot_general(
                left, other, (((0,), (0,)), ((), ())), preferred_element_type=f32
            )
            buf[at, :] = (w[at, :].astype(f32) + step_coef * term).astype(bf16)
            here = pl.ds(i * step, step)
            copies.append(pltpu.make_async_copy(buf.at[here], out.at[here], sem.at[i]))
            copies[-1].start()
        for c in copies:
            c.wait()

    return call(
        kernel,
        [((rows, cols), weight.dtype)],
        [SMEM] + [VMEM] * (n + 2),
        "update",
        [pltpu.VMEM((rows, cols), bf16), pltpu.SemaphoreType.DMA((parts,))],
        out_specs=(ANY,),
    )(where, *factors, right, weight)[0]


def on_device(
    tokens,
    gate_weight,
    up_weight,
    down_weight,
    gate_left,
    gate_right,
    up_left,
    up_right,
    down_left,
    down_right,
    fitness,
):
    rows, deep = tokens.shape
    own = gate_left.shape[0]
    members = fitness.shape[0]
    per = rows // own
    d_model = deep * lax.axis_size("narrow")
    d_hidden = gate_weight.shape[1] * lax.axis_size("wide")
    w = lax.axis_index("wide")
    where = jnp.stack(
        [lax.axis_index("narrow") % 2, w // (NH * NZ), (w // NZ) % NH, w % NZ]
    ).astype(jnp.int32)

    packed, weighted = prepare(where, fitness, tokens, gate_left, up_left, down_right)

    over = from_h(packed, "tokens_xhi")
    weighted_over = from_h(weighted, "factors_xhi")
    gate_weight, up_weight = resident(after(gate_weight, packed), up_weight)
    mine, theirs = split_halves(where, after(packed, gate_weight), over)
    block = stack([mine] + from_core([theirs], "tokens_core"))
    parts = [block] + [early(block, d, f"tokens_early{d}") for d in STEPS[1:]]
    (down_weight,) = resident(after(down_weight, block))
    line = stack([after(block, down_weight, weighted_over)] + parts[1:], 2)
    lines = {0: line, **{d: late(line, d, f"tokens_late{d}") for d in STEPS[1:3]}}
    n = line.shape[0] // 2

    def project(d, x, *before):
        others = after(from_core(cut(x, n, 4), f"rows_core{d}"), *before)
        return gate_up(where, d, own, per, x, others, gate_weight, up_weight, gate_right, up_right)

    def activate(mine, other, pieces, name):
        return hidden_units(mine, other, d_model**-0.5, pieces, name)

    def contract(steps, hidden, others, dtype, pieces, name):
        kept, sent = down(
            where, steps, own, per, hidden, others, down_weight, down_left, dtype, pieces, name
        )
        return kept, from_core(sent, f"{name}_core")

    keep0, send0 = project(0, line)
    mine0, coarse0 = add_both([keep0], from_core(send0, "sums_core0"), "add0")
    lines[2] = late(after(line, lines[1], coarse0), 2, "tokens_late2")
    keep1, send1 = project(1, after(lines[1], coarse0))
    got1 = from_core(send1, "sums_core1")
    keep3, send3 = project(3, after(lines[3], keep1), got1)
    mine13, coarse13 = add_both(
        [keep1, keep3], got1 + from_core(send3, "sums_core3"), "add13"
    )
    other13 = from_x(coarse13, "sums_x13")

    weighted = after(jnp.concatenate([weighted, weighted_over], 0), coarse13)
    factor_line = stack([weighted] + [early(weighted, d, f"factors_early{d}") for d in STEPS[1:]])

    keep2, send2 = project(2, after(lines[2], coarse13))
    mine2, coarse2 = add_both([keep2], from_core(send2, "sums_core2"), "add2")
    other2 = from_x(coarse2, "sums_x2")
    factors = {0: factor_line, **{d: late(factor_line, d, f"factors_late{d}") for d in STEPS[1:]}}

    hidden13 = activate(after(mine13, coarse2), other13, 4, "hidden13")
    hidden13_o = from_core(hidden13, "hidden_core13")
    kept, sent = contract([1, 3], hidden13, hidden13_o, bf16, 2, "down13")
    coarse0 = after(coarse0, kept)
    kept = after(kept, other2, factors[1], factors[3])
    out1, out3 = stack(kept[:2] + sent[:2]), stack(kept[2:] + sent[2:])
    sum1, sum3 = late(out1, 3, "out_late1"), late(out3, 1, "out_late3")

    other0 = from_x(coarse0, "sums_x0")

    hidden2 = activate(after(mine2, out1, out3), other2, 2, "hidden2")
    kept, sent = contract([2], hidden2, from_core(hidden2, "hidden_core2"), bf16, 4, "down2")
    out2 = stack(after(kept, factors[2]) + sent)
    sum2 = late(out2, 2, "out_late2")

    step_coef = step_size / math.sqrt(members)
    factors = after([factors[d] for d in STEPS], out2)
    new_gate = update(where, own, factors, 0, gate_right, gate_weight, step_coef)

    hidden0 = activate(after(mine0, new_gate), other0, 2, "hidden0")
    hidden0_o = from_core(hidden0, "hidden_core0")
    kept0, sent0 = contract([0], after(hidden0, sum1), hidden0_o, f32, 4, "down0")

    pieces = fold(kept0 + sent0, [sum1, sum3, sum2], len(STEPS))
    got = [early(p, 4 - d, f"out_early{d}") for p, d in zip(pieces[1:], STEPS[1:])]
    factors = after(factors, pieces[0])
    new_up = update(where, own, factors, deep, up_right, up_weight, step_coef)
    ours, away = fold([after(pieces[0], new_up)], got, NH)
    factors = after(factors, ours)
    new_down = update(
        where, own, factors, 2 * deep, down_left, down_weight, step_coef, True
    )
    both = fold([after(ours, new_down)], [from_h(away, "out_xhi")], 1)[0]
    half = rows // 2
    (theirs,) = from_core([both[half:]], "out_core")
    mlp_out = finish(where, both[:half], theirs, down_right, d_hidden**-0.5)
    return (mlp_out, new_gate, new_up, new_down)


def solution(mesh):
    placed = (
        P("wide", "narrow"),
        P("narrow", "wide"),
        P("narrow", "wide"),
        P("wide", "narrow"),
        P("wide", "narrow"),
        P(None, "wide"),
        P("wide", "narrow"),
        P(None, "wide"),
        P(None, "wide"),
        P("wide", "narrow"),
        P(),
    )
    return jax.shard_map(
        on_device,
        mesh=mesh,
        in_specs=placed,
        out_specs=(
            P("wide", "narrow"),
            P("narrow", "wide"),
            P("narrow", "wide"),
            P("wide", "narrow"),
        ),
        check_vma=False,
    )
```

```python
import math

import jax
import jax.numpy as jnp
from jax import lax
from jax.experimental import pallas as pl
from jax.experimental.pallas import tpu as pltpu
from jax.sharding import PartitionSpec as P

NY, NH, NZ = 4, 2, 4
STEPS = (0, 1, 3, 2)
LANES = 128
noise_scale = 0.5
step_size = 0.5

f32, bf16 = jnp.float32, jnp.bfloat16
SCOPED = 12 << 20
COST = pl.CostEstimate(flops=1000, bytes_accessed=1000, transcendentals=0)


def wide_index(y, h, z):
    return (y % NY) * (NH * NZ) + (h % NH) * NZ + z % NZ


def wide_perm(dy, dh, dz):
    return [
        (wide_index(y + dy, h + dh, z + dz), wide_index(y, h, z))
        for y in range(NY)
        for h in range(NH)
        for z in range(NZ)
    ]


def by_core(first, second):
    return [
        (4 * i + n, 4 * j + n)
        for n in range(4)
        for i, j in (second if n % 2 else first)
    ]


def early(x, d, name):
    pairs = by_core(wide_perm(0, 0, d), wide_perm(d, 0, 0))
    with jax.named_scope(name):
        return lax.ppermute(x, ("wide", "narrow"), pairs)


def late(x, d, name):
    pairs = by_core(wide_perm(d, 0, 0), wide_perm(0, 0, d))
    with jax.named_scope(name):
        return lax.ppermute(x, ("wide", "narrow"), pairs)


def from_h(x, name):
    with jax.named_scope(name):
        return lax.ppermute(x, "wide", wide_perm(0, 1, 0))


def from_core(pieces, name):
    with jax.named_scope(name):
        pairs = [(n, n ^ 1) for n in range(4)]
        return [lax.ppermute(p, "narrow", pairs) for p in pieces]


def from_x(x, name):
    with jax.named_scope(name):
        return lax.ppermute(x, "narrow", [(n, n ^ 2) for n in range(4)])


def after(x, *others):
    return lax.optimization_barrier((x, *others))[0]


VMEM = pl.BlockSpec(memory_space=pltpu.VMEM)
SMEM = pl.BlockSpec(memory_space=pltpu.SMEM)
ANY = pl.BlockSpec(memory_space=pl.ANY)


def call(kernel, outs, in_specs, name, scratch=(), out_specs=None):
    if out_specs is None:
        out_specs = tuple(VMEM for _ in outs)
        out_shape = tuple(pltpu.VMEM(s, t) for s, t in outs)
    else:
        out_shape = tuple(jax.ShapeDtypeStruct(s, t) for s, t in outs)
    return pl.pallas_call(
        kernel,
        out_shape=out_shape,
        in_specs=in_specs,
        out_specs=out_specs,
        scratch_shapes=list(scratch),
        compiler_params=pltpu.CompilerParams(vmem_limit_bytes=SCOPED),
        cost_estimate=COST,
        name=name,
    )


def in_hbm(x):
    return pltpu.with_memory_space_constraint(x, pltpu.HBM)


def steps_of(r):
    return r ^ (r >> 1)


def one_hot(m, members):
    return (m == lax.broadcasted_iota(jnp.int32, m.shape, 1)).astype(bf16)


def members_of(where, d, part, rows, half, own, per, members):
    r = lax.broadcasted_iota(jnp.int32, (rows, members), 0)
    s = steps_of(r // (NH * half))
    y = where[1] + jnp.where(part == 0, d, s)
    z = where[3] + jnp.where(part == 0, s, d)
    m = wide_index(y, where[2] + r // half, z) * own + (r % half) // per + part * (own // 2)
    return one_hot(m, members)


def gathered_order(where, own, members):
    r = lax.broadcasted_iota(jnp.int32, (members, members), 0)
    late_step, early_step = steps_of(r // (NZ * NH * own)), steps_of(r // (NH * own) % NZ)
    first = where[0] == 0
    y = where[1] + jnp.where(first, late_step, early_step)
    z = where[3] + jnp.where(first, early_step, late_step)
    return one_hot(wide_index(y, where[2] + r // own, z) * own + r % own, members)


def prepare(where, fitness, tokens, gate_left, up_left, down_right):
    rows, deep = tokens.shape
    own = gate_left.shape[0]
    arrays = (tokens, gate_left, up_left, down_right, fitness)
    n = len(arrays)

    def kernel(where, *refs):
        sources, (packed, weighted), (*here, sem) = refs[:n], refs[n : n + 2], refs[n + 2 :]
        tok, gl, ul, dr, fitness = here
        copies = [
            pltpu.make_async_copy(a, b, sem.at[i]) for i, (a, b) in enumerate(zip(sources, here))
        ]
        for c in copies:
            c.start()
        for c in copies:
            c.wait()
        packed[:, :deep] = tok[...]
        r = lax.broadcasted_iota(jnp.int32, (rows, own), 0)
        whose = r // (rows // own) == lax.broadcasted_iota(jnp.int32, (rows, own), 1)
        lane = lax.broadcasted_iota(jnp.int32, (rows, LANES), 1)
        extra = jnp.zeros((rows, LANES), f32)
        for c, left in enumerate((gl, ul)):
            dots = lax.dot_general(
                tok[...], left[...], (((1,), (1,)), ((), ())), preferred_element_type=f32
            )
            proj = jnp.sum(jnp.where(whose, dots, 0.0), 1, keepdims=True)
            high = proj.astype(bf16).astype(f32)
            extra = jnp.where(lane == 2 * c, high, extra)
            extra = jnp.where(lane == 2 * c + 1, proj - high, extra)
        packed[:, deep:] = extra.astype(bf16)
        w = (where[1] * NH + where[2]) * NZ + where[3]
        r = lax.broadcasted_iota(jnp.int32, (own, LANES), 0)
        fit = jnp.zeros((own, LANES), f32)
        for i in range(own):
            fit = jnp.where(r == i, fitness[w * own + i], fit)
        for c, left in enumerate((gl, ul, dr)):
            weighted[:, c * deep : (c + 1) * deep] = (
                left[...].astype(f32) * fit[:, :1]
            ).astype(bf16)

    return call(
        kernel,
        [((rows, deep + LANES), bf16), ((own, 3 * deep), bf16)],
        [SMEM] + [ANY] * n,
        "prepare",
        [pltpu.VMEM(v.shape, v.dtype) for v in arrays[:4]]
        + [pltpu.SMEM(fitness.shape, f32), pltpu.SemaphoreType.DMA((n,))],
    )(where, *[in_hbm(v) for v in arrays])


def resident(*arrays):
    n, parts = len(arrays), 4

    def kernel(*refs):
        src, dst, sem = refs[:n], refs[n : 2 * n], refs[2 * n]
        copies = []
        for i in range(n):
            step = src[i].shape[0] // parts
            for q in range(parts):
                rows = pl.ds(q * step, step)
                copies.append(
                    pltpu.make_async_copy(src[i].at[rows], dst[i].at[rows], sem.at[i, q])
                )
        for c in copies:
            c.start()
        for c in copies:
            c.wait()

    return call(
        kernel,
        [(v.shape, v.dtype) for v in arrays],
        [ANY] * n,
        "resident",
        [pltpu.SemaphoreType.DMA((n, parts))],
    )(*[in_hbm(v) for v in arrays])


def split_halves(where, own, over):
    rows, cols = own.shape
    half = rows // 2

    def kernel(where, own, over, mine, theirs):
        a = jnp.concatenate([own[:half, :], over[:half, :]], 0)
        b = jnp.concatenate([own[half:, :], over[half:, :]], 0)
        first = where[0] == 0
        mine[...] = jnp.where(first, a, b)
        theirs[...] = jnp.where(first, b, a)

    return call(kernel, [((rows, cols), own.dtype)] * 2, [SMEM, VMEM, VMEM], "split_halves")(
        where, own, over
    )


def stack(parts, pieces=1):
    cols, n = parts[0].shape[1], len(parts)

    def kernel(*refs):
        at = 0
        for q in range(pieces):
            for ref in refs[:n]:
                step = ref.shape[0] // pieces
                refs[n][at : at + step, :] = ref[q * step : (q + 1) * step, :]
                at += step

    rows = sum(p.shape[0] for p in parts)
    return call(kernel, [((rows, cols), parts[0].dtype)], [VMEM] * n, "stack")(*parts)[0]


def cut(x, start, count):
    rows, cols = x.shape
    step = (rows - start) // count

    def kernel(x, *outs):
        for i, out in enumerate(outs):
            out[...] = x[start + i * step : start + (i + 1) * step, :]

    return call(kernel, [((step, cols), x.dtype)] * count, [VMEM], "cut")(x)


def whole(refs):
    return jnp.concatenate([r[...] for r in refs], 0)


def gate_up(count, where, d, own, per, x, others, wg, wu, rg, ru):
    rows, deep, n = x.shape[0] // 2, wg.shape[0], len(others)
    cols, members = wg.shape[1], rg.shape[0]
    tile, step = 2 * LANES, rows // count

    def kernel(where, x, *refs):
        xo, (wg, wu, rg, ru, keep), send = refs[:n], refs[n : n + 5], refs[n + 5 :]
        xs = jnp.concatenate([x[:rows, :deep]] + [r[:, :deep] for r in xo], 0)
        proj = jnp.concatenate([x[:rows, deep:]] + [r[:, deep:] for r in xo], 0).astype(f32)
        pick = jnp.concatenate(
            [
                members_of(where, d, part, rows, own * per // 2, own, per, members)
                for part in (where[0], 1 - where[0])
            ],
            0,
        )
        for j, (w, r) in enumerate(((wg, rg), (wu, ru))):
            scale = noise_scale * (proj[:, 2 * j : 2 * j + 1] + proj[:, 2 * j + 1 : 2 * j + 2])
            for t in range(0, cols, tile):
                at = slice(t, min(cols, t + tile))
                prod = jnp.dot(xs, w[:, at], preferred_element_type=f32)
                prod += scale * jnp.dot(pick, r[:, at], preferred_element_type=f32)
                to = slice(j * cols + at.start, j * cols + at.stop)
                keep[:, to] = prod[:rows]
                for i, out in enumerate(send):
                    out[:, to] = prod[rows + i * step : rows + (i + 1) * step]

    keep, *send = call(
        kernel,
        [((rows, 2 * cols), f32)] + [((step, 2 * cols), f32)] * count,
        [SMEM] + [VMEM] * (n + 5),
        f"gate_up{d}",
    )(where, x, *others, wg, wu, rg, ru)
    return keep, send


def add_both(kept, pieces, name):
    n, cols = len(kept), kept[0].shape[1]
    rows = sum(a.shape[0] for a in kept)

    def kernel(*refs):
        total, coarse = refs[-2:]
        s = whole(refs[:n]) + whole(refs[n:-2])
        total[...] = s
        coarse[...] = s.astype(bf16)

    return call(
        kernel, [((rows, cols), f32), ((rows, cols), bf16)], [VMEM] * (n + len(pieces)), name
    )(*kept, *pieces)


def hidden_units(mine, other, scale, pieces, name):
    rows, cols = mine.shape
    n, step = cols // 2, rows // pieces

    def kernel(mine, other, *outs):
        gate = (mine[:, :n] + other[:, :n].astype(f32)) * scale
        up = (mine[:, n:] + other[:, n:].astype(f32)) * scale
        hidden = (jax.nn.silu(gate) * up).astype(bf16)
        for i, out in enumerate(outs):
            out[...] = hidden[i * step : (i + 1) * step]

    return list(call(kernel, [((step, n), bf16)] * pieces, [VMEM, VMEM], name)(mine, other))


def down(where, steps, own, per, mine, others, wd, left, dtype, pieces, name):
    n, rows = len(mine), sum(m.shape[0] for m in mine)
    cols = wd.shape[1]
    each, count = rows // len(steps), pieces * len(steps)
    tile, step = 4 * LANES, rows // count

    def kernel(where, *refs):
        hm, ho, (wd, left), outs = refs[:n], refs[n : 2 * n], refs[2 * n : 2 * n + 2], refs[2 * n + 2 :]
        both = jnp.concatenate([whole(hm), whole(ho)], 0)
        pick = jnp.concatenate(
            [
                members_of(where, d, part, each, own * per // 2, own, per, left.shape[0])
                for part in (where[0], 1 - where[0])
                for d in steps
            ],
            0,
        )
        rows_left = jnp.dot(pick, left[...], preferred_element_type=f32)
        proj = jnp.sum(both.astype(f32) * rows_left, axis=1, keepdims=True)
        proj = jnp.broadcast_to(proj, (2 * rows, LANES))
        for t in range(0, cols + LANES, tile):
            at = slice(t, min(cols, t + tile)) if t < cols else slice(cols, cols + LANES)
            prod = jnp.dot(both, wd[:, at], preferred_element_type=f32) if t < cols else proj
            for i, out in enumerate(outs):
                out[:, at] = prod[i * step : (i + 1) * step].astype(dtype)

    outs = call(
        kernel,
        [((step, cols + LANES), dtype)] * (2 * count),
        [SMEM] + [VMEM] * (2 * n + 2),
        name,
    )(where, *mine, *others, wd, left)
    return list(outs[:count]), list(outs[count:])


def fold(base, got, pieces):
    rows, cols = got[0].shape
    half, step = rows // 2, rows // 2 // pieces
    n = len(base)

    def kernel(*refs):
        base_refs, got_refs, outs = refs[:n], refs[n : n + len(got)], refs[n + len(got) :]
        each = rows // n
        for c in range(pieces):
            for q in range(2):
                at = q * half + c * step
                b = base_refs[at // each]
                s = b[at % each : at % each + step, :].astype(f32)
                for g in got_refs:
                    s += g[at : at + step, :].astype(f32)
                outs[c][q * step : (q + 1) * step, :] = s.astype(outs[c].dtype)

    return call(
        kernel,
        [((2 * step, cols), bf16 if c else f32) for c in range(pieces)],
        [VMEM] * (n + len(got)),
        "fold",
    )(*base, *got)


def finish(where, mine, theirs, down_right, scale):
    half, deep = mine.shape[0], down_right.shape[1]
    rows, own = 2 * half, down_right.shape[0]

    def kernel(where, mine, theirs, right, out):
        first = where[0] == 0
        a = jnp.where(first, mine[...], theirs[...])
        b = jnp.where(first, theirs[...], mine[...])
        total = jnp.concatenate([a, b], 0)
        r = lax.broadcasted_iota(jnp.int32, (rows, own), 0) // (rows // own)
        pick = (r == lax.broadcasted_iota(jnp.int32, (rows, own), 1)).astype(bf16)
        right_rows = jnp.dot(pick, right[...], preferred_element_type=f32)
        shaped = total[:, :deep] + noise_scale * total[:, deep : deep + 1] * right_rows
        out[...] = (shaped * scale).astype(out.dtype)

    return call(
        kernel,
        [((rows, deep), bf16)],
        [SMEM] + [VMEM] * 3,
        "finish",
        out_specs=(VMEM,),
    )(where, mine, theirs, down_right)[0]


def update(where, own, factors, start, right, weight, step_coef, transposed=False):
    rows, cols = weight.shape
    members, n = right.shape[0], len(factors)
    parts = 4 if rows % (4 * LANES) == 0 else max(1, rows // LANES)
    step = rows // parts

    def kernel(where, *refs):
        pieces, (r, w, out, buf, sem) = refs[:n], refs[n:]
        order = gathered_order(where, own, members)
        moved = jnp.dot(order, r[...], preferred_element_type=f32).astype(bf16)
        copies = []
        for i in range(parts):
            at = slice(i * step, (i + 1) * step)
            take = slice(start, start + cols) if transposed else slice(start + i * step, start + (i + 1) * step)
            side = jnp.concatenate([p[:, take] for p in pieces], 0)
            left, other = (moved[:, at], side) if transposed else (side, moved)
            term = lax.dot_general(
                left, other, (((0,), (0,)), ((), ())), preferred_element_type=f32
            )
            buf[at, :] = (w[at, :].astype(f32) + step_coef * term).astype(bf16)
            here = pl.ds(i * step, step)
            copies.append(pltpu.make_async_copy(buf.at[here], out.at[here], sem.at[i]))
            copies[-1].start()
        for c in copies:
            c.wait()

    return call(
        kernel,
        [((rows, cols), weight.dtype)],
        [SMEM] + [VMEM] * (n + 2),
        "update",
        [pltpu.VMEM((rows, cols), bf16), pltpu.SemaphoreType.DMA((parts,))],
        out_specs=(ANY,),
    )(where, *factors, right, weight)[0]


def on_device(
    tokens,
    gate_weight,
    up_weight,
    down_weight,
    gate_left,
    gate_right,
    up_left,
    up_right,
    down_left,
    down_right,
    fitness,
):
    rows, deep = tokens.shape
    own = gate_left.shape[0]
    members = fitness.shape[0]
    per = rows // own
    d_model = deep * lax.axis_size("narrow")
    d_hidden = gate_weight.shape[1] * lax.axis_size("wide")
    w = lax.axis_index("wide")
    where = jnp.stack(
        [lax.axis_index("narrow") % 2, w // (NH * NZ), (w // NZ) % NH, w % NZ]
    ).astype(jnp.int32)

    packed, weighted = prepare(where, fitness, tokens, gate_left, up_left, down_right)

    over = from_h(packed, "tokens_xhi")
    weighted_over = from_h(weighted, "factors_xhi")
    gate_weight, up_weight = resident(after(gate_weight, packed), up_weight)
    mine, theirs = split_halves(where, after(packed, gate_weight), over)
    block = stack([mine] + from_core([theirs], "tokens_core"))
    parts = [block] + [early(block, d, f"tokens_early{d}") for d in STEPS[1:]]
    (down_weight,) = resident(after(down_weight, block))
    line = stack([after(block, down_weight, weighted_over)] + parts[1:], 2)
    lines = {0: line, **{d: late(line, d, f"tokens_late{d}") for d in STEPS[1:3]}}
    n = line.shape[0] // 2

    def exchange(d, x):
        return from_core(cut(x, n, 4), f"rows_core{d}")

    def project(d, x, others, count=4):
        return gate_up(count, where, d, own, per, x, others, gate_weight, up_weight, gate_right, up_right)

    def activate(mine, other, pieces, name):
        return hidden_units(mine, other, d_model**-0.5, pieces, name)

    def contract(steps, hidden, others, dtype, pieces, name):
        kept, sent = down(
            where, steps, own, per, hidden, others, down_weight, down_left, dtype, pieces, name
        )
        return kept, from_core(sent, f"{name}_core")

    keep0, send0 = project(0, line, exchange(0, line))
    mine0, coarse0 = add_both([keep0], from_core(send0, "sums_core0"), "add0")
    lines[2] = late(after(lines[1], coarse0), 1, "tokens_late2")
    x = after(lines[1], coarse0)
    others1, others3 = exchange(1, x), exchange(3, after(lines[3], coarse0))
    keep1, send1 = project(1, x, after(others1, others3), 2)
    keep3, send3 = project(3, after(lines[3], keep1), others3)
    got1 = from_core(send1, "sums_core1")
    mine13, coarse13 = add_both(
        [keep1, keep3], got1 + from_core(send3, "sums_core3"), "add13"
    )
    other13 = from_x(coarse13, "sums_x13")

    x = after(lines[2], coarse13)
    others2 = exchange(2, x)

    weighted = after(jnp.concatenate([weighted, weighted_over], 0), others2)
    factor_line = stack([weighted] + [early(weighted, d, f"factors_early{d}") for d in STEPS[1:]])

    keep2, send2 = project(2, x, others2)
    mine2, coarse2 = add_both([keep2], from_core(send2, "sums_core2"), "add2")
    other2 = from_x(coarse2, "sums_x2")
    factors = {0: factor_line, **{d: late(factor_line, d, f"factors_late{d}") for d in STEPS[1:]}}

    hidden13 = activate(after(mine13, coarse2), other13, 2, "hidden13")
    hidden13_o = from_core(hidden13, "hidden_core13")
    kept, sent = contract([1, 3], hidden13, hidden13_o, bf16, 2, "down13")
    coarse0 = after(coarse0, kept)
    kept = after(kept, other2, factors[1], factors[3])
    out1, out3 = stack(kept[:2] + sent[:2]), stack(kept[2:] + sent[2:])
    sum1, sum3 = late(out1, 3, "out_late1"), late(out3, 1, "out_late3")

    other0 = from_x(coarse0, "sums_x0")

    hidden2 = activate(after(mine2, out1, out3), other2, 2, "hidden2")
    kept, sent = contract([2], hidden2, from_core(hidden2, "hidden_core2"), bf16, 4, "down2")
    out2 = stack(after(kept, factors[2]) + sent)
    sum2 = late(out2, 2, "out_late2")

    hidden0 = activate(after(mine0, out2), other0, 2, "hidden0")
    hidden0_o = from_core(hidden0, "hidden_core0")
    kept0, sent0 = down(
        where, [0], own, per, hidden0, hidden0_o, down_weight, down_left, f32, 2, "down0"
    )
    sent0 = from_core(after(sent0, sum1, sum3), "down0_core")

    pieces = fold(kept0 + sent0, [sum1, sum3, sum2], len(STEPS))
    got = [early(p, 4 - d, f"out_early{d}") for p, d in zip(pieces[1:], STEPS[1:])]

    step_coef = step_size / math.sqrt(members)
    factors = after([factors[d] for d in STEPS], pieces[0])
    new_gate = update(where, own, factors, 0, gate_right, gate_weight, step_coef)
    new_up = update(where, own, factors, deep, up_right, up_weight, step_coef)
    ours, away = fold([after(pieces[0], new_gate, new_up)], got, NH)
    factors = after(factors, ours)
    new_down = update(
        where, own, factors, 2 * deep, down_left, down_weight, step_coef, True
    )
    both = fold([after(ours, new_down)], [from_h(away, "out_xhi")], 1)[0]
    half = rows // 2
    (theirs,) = from_core([both[half:]], "out_core")
    mlp_out = finish(where, both[:half], theirs, down_right, d_hidden**-0.5)
    return (mlp_out, new_gate, new_up, new_down)


def solution(mesh):
    placed = (
        P("wide", "narrow"),
        P("narrow", "wide"),
        P("narrow", "wide"),
        P("wide", "narrow"),
        P("wide", "narrow"),
        P(None, "wide"),
        P("wide", "narrow"),
        P(None, "wide"),
        P(None, "wide"),
        P("wide", "narrow"),
        P(),
    )
    return jax.shard_map(
        on_device,
        mesh=mesh,
        in_specs=placed,
        out_specs=(
            P("wide", "narrow"),
            P("narrow", "wide"),
            P("narrow", "wide"),
            P("wide", "narrow"),
        ),
        check_vma=False,
    )
```

```python
import math

import jax
import jax.numpy as jnp
from jax import lax
from jax.experimental import pallas as pl
from jax.experimental.pallas import tpu as pltpu
from jax.sharding import PartitionSpec as P

NY, NH, NZ = 4, 2, 4
STEPS = (0, 1, 3, 2)
LANES = 128
noise_scale = 0.5
step_size = 0.5

f32, bf16 = jnp.float32, jnp.bfloat16
SCOPED = 12 << 20
COST = pl.CostEstimate(flops=1000, bytes_accessed=1000, transcendentals=0)


def wide_index(y, h, z):
    return (y % NY) * (NH * NZ) + (h % NH) * NZ + z % NZ


def wide_perm(dy, dh, dz):
    return [
        (wide_index(y + dy, h + dh, z + dz), wide_index(y, h, z))
        for y in range(NY)
        for h in range(NH)
        for z in range(NZ)
    ]


def by_core(first, second):
    return [
        (4 * i + n, 4 * j + n)
        for n in range(4)
        for i, j in (second if n % 2 else first)
    ]


def early(x, d, name):
    pairs = by_core(wide_perm(0, 0, d), wide_perm(d, 0, 0))
    with jax.named_scope(name):
        return lax.ppermute(x, ("wide", "narrow"), pairs)


def late(x, d, name):
    pairs = by_core(wide_perm(d, 0, 0), wide_perm(0, 0, d))
    with jax.named_scope(name):
        return lax.ppermute(x, ("wide", "narrow"), pairs)


def from_h(x, name):
    with jax.named_scope(name):
        return lax.ppermute(x, "wide", wide_perm(0, 1, 0))


def from_core(pieces, name):
    with jax.named_scope(name):
        pairs = [(n, n ^ 1) for n in range(4)]
        return [lax.ppermute(p, "narrow", pairs) for p in pieces]


def from_x(x, name):
    with jax.named_scope(name):
        return lax.ppermute(x, "narrow", [(n, n ^ 2) for n in range(4)])


def after(x, *others):
    return lax.optimization_barrier((x, *others))[0]


VMEM = pl.BlockSpec(memory_space=pltpu.VMEM)
SMEM = pl.BlockSpec(memory_space=pltpu.SMEM)
ANY = pl.BlockSpec(memory_space=pl.ANY)


def call(kernel, outs, in_specs, name, scratch=(), out_specs=None):
    if out_specs is None:
        out_specs = tuple(VMEM for _ in outs)
        out_shape = tuple(pltpu.VMEM(s, t) for s, t in outs)
    else:
        out_shape = tuple(jax.ShapeDtypeStruct(s, t) for s, t in outs)
    return pl.pallas_call(
        kernel,
        out_shape=out_shape,
        in_specs=in_specs,
        out_specs=out_specs,
        scratch_shapes=list(scratch),
        compiler_params=pltpu.CompilerParams(vmem_limit_bytes=SCOPED),
        cost_estimate=COST,
        name=name,
    )


def in_hbm(x):
    return pltpu.with_memory_space_constraint(x, pltpu.HBM)


def steps_of(r):
    return r ^ (r >> 1)


def one_hot(m, members):
    return (m == lax.broadcasted_iota(jnp.int32, m.shape, 1)).astype(bf16)


def members_of(where, d, part, rows, half, own, per, members):
    r = lax.broadcasted_iota(jnp.int32, (rows, members), 0)
    s = steps_of(r // (NH * half))
    y = where[1] + jnp.where(part == 0, d, s)
    z = where[3] + jnp.where(part == 0, s, d)
    m = wide_index(y, where[2] + r // half, z) * own + (r % half) // per + part * (own // 2)
    return one_hot(m, members)


def gathered_order(where, own, members):
    r = lax.broadcasted_iota(jnp.int32, (members, members), 0)
    late_step, early_step = steps_of(r // (NZ * NH * own)), steps_of(r // (NH * own) % NZ)
    first = where[0] == 0
    y = where[1] + jnp.where(first, late_step, early_step)
    z = where[3] + jnp.where(first, early_step, late_step)
    return one_hot(wide_index(y, where[2] + r // own, z) * own + r % own, members)


def prepare(where, fitness, tokens, gate_left, up_left, down_right):
    rows, deep = tokens.shape
    own = gate_left.shape[0]
    arrays = (tokens, gate_left, up_left, down_right, fitness)
    n = len(arrays)

    def kernel(where, *refs):
        sources, (packed, weighted), (*here, sem) = refs[:n], refs[n : n + 2], refs[n + 2 :]
        tok, gl, ul, dr, fitness = here
        copies = [
            pltpu.make_async_copy(a, b, sem.at[i]) for i, (a, b) in enumerate(zip(sources, here))
        ]
        for c in copies:
            c.start()
        for c in copies:
            c.wait()
        packed[:, :deep] = tok[...]
        r = lax.broadcasted_iota(jnp.int32, (rows, own), 0)
        whose = r // (rows // own) == lax.broadcasted_iota(jnp.int32, (rows, own), 1)
        lane = lax.broadcasted_iota(jnp.int32, (rows, LANES), 1)
        extra = jnp.zeros((rows, LANES), f32)
        for c, left in enumerate((gl, ul)):
            dots = lax.dot_general(
                tok[...], left[...], (((1,), (1,)), ((), ())), preferred_element_type=f32
            )
            proj = jnp.sum(jnp.where(whose, dots, 0.0), 1, keepdims=True)
            high = proj.astype(bf16).astype(f32)
            extra = jnp.where(lane == 2 * c, high, extra)
            extra = jnp.where(lane == 2 * c + 1, proj - high, extra)
        packed[:, deep:] = extra.astype(bf16)
        w = (where[1] * NH + where[2]) * NZ + where[3]
        r = lax.broadcasted_iota(jnp.int32, (own, LANES), 0)
        fit = jnp.zeros((own, LANES), f32)
        for i in range(own):
            fit = jnp.where(r == i, fitness[w * own + i], fit)
        for c, left in enumerate((gl, ul, dr)):
            weighted[:, c * deep : (c + 1) * deep] = (
                left[...].astype(f32) * fit[:, :1]
            ).astype(bf16)

    return call(
        kernel,
        [((rows, deep + LANES), bf16), ((own, 3 * deep), bf16)],
        [SMEM] + [ANY] * n,
        "prepare",
        [pltpu.VMEM(v.shape, v.dtype) for v in arrays[:4]]
        + [pltpu.SMEM(fitness.shape, f32), pltpu.SemaphoreType.DMA((n,))],
    )(where, *[in_hbm(v) for v in arrays])


def resident(*arrays):
    n, parts = len(arrays), 4

    def kernel(*refs):
        src, dst, sem = refs[:n], refs[n : 2 * n], refs[2 * n]
        copies = []
        for i in range(n):
            step = src[i].shape[0] // parts
            for q in range(parts):
                rows = pl.ds(q * step, step)
                copies.append(
                    pltpu.make_async_copy(src[i].at[rows], dst[i].at[rows], sem.at[i, q])
                )
        for c in copies:
            c.start()
        for c in copies:
            c.wait()

    return call(
        kernel,
        [(v.shape, v.dtype) for v in arrays],
        [ANY] * n,
        "resident",
        [pltpu.SemaphoreType.DMA((n, parts))],
    )(*[in_hbm(v) for v in arrays])


def split_halves(where, own, over):
    rows, cols = own.shape
    half = rows // 2

    def kernel(where, own, over, mine, theirs):
        a = jnp.concatenate([own[:half, :], over[:half, :]], 0)
        b = jnp.concatenate([own[half:, :], over[half:, :]], 0)
        first = where[0] == 0
        mine[...] = jnp.where(first, a, b)
        theirs[...] = jnp.where(first, b, a)

    return call(kernel, [((rows, cols), own.dtype)] * 2, [SMEM, VMEM, VMEM], "split_halves")(
        where, own, over
    )


def stack(parts, pieces=1):
    cols, n = parts[0].shape[1], len(parts)

    def kernel(*refs):
        at = 0
        for q in range(pieces):
            for ref in refs[:n]:
                step = ref.shape[0] // pieces
                refs[n][at : at + step, :] = ref[q * step : (q + 1) * step, :]
                at += step

    rows = sum(p.shape[0] for p in parts)
    return call(kernel, [((rows, cols), parts[0].dtype)], [VMEM] * n, "stack")(*parts)[0]


def cut(x, start, count):
    rows, cols = x.shape
    step = (rows - start) // count

    def kernel(x, *outs):
        for i, out in enumerate(outs):
            out[...] = x[start + i * step : start + (i + 1) * step, :]

    return call(kernel, [((step, cols), x.dtype)] * count, [VMEM], "cut")(x)


def whole(refs):
    return jnp.concatenate([r[...] for r in refs], 0)


def gate_up(count, where, d, own, per, x, others, wg, wu, rg, ru):
    rows, deep, n = x.shape[0] // 2, wg.shape[0], len(others)
    cols, members = wg.shape[1], rg.shape[0]
    tile, step = 2 * LANES, rows // count

    def kernel(where, x, *refs):
        xo, (wg, wu, rg, ru, keep), send = refs[:n], refs[n : n + 5], refs[n + 5 :]
        xs = jnp.concatenate([x[:rows, :deep]] + [r[:, :deep] for r in xo], 0)
        proj = jnp.concatenate([x[:rows, deep:]] + [r[:, deep:] for r in xo], 0).astype(f32)
        pick = jnp.concatenate(
            [
                members_of(where, d, part, rows, own * per // 2, own, per, members)
                for part in (where[0], 1 - where[0])
            ],
            0,
        )
        for j, (w, r) in enumerate(((wg, rg), (wu, ru))):
            scale = noise_scale * (proj[:, 2 * j : 2 * j + 1] + proj[:, 2 * j + 1 : 2 * j + 2])
            for t in range(0, cols, tile):
                at = slice(t, min(cols, t + tile))
                prod = jnp.dot(xs, w[:, at], preferred_element_type=f32)
                prod += scale * jnp.dot(pick, r[:, at], preferred_element_type=f32)
                to = slice(j * cols + at.start, j * cols + at.stop)
                keep[:, to] = prod[:rows]
                for i, out in enumerate(send):
                    out[:, to] = prod[rows + i * step : rows + (i + 1) * step]

    keep, *send = call(
        kernel,
        [((rows, 2 * cols), f32)] + [((step, 2 * cols), f32)] * count,
        [SMEM] + [VMEM] * (n + 5),
        f"gate_up{d}",
    )(where, x, *others, wg, wu, rg, ru)
    return keep, send


def add_both(kept, pieces, name):
    n, cols = len(kept), kept[0].shape[1]
    rows = sum(a.shape[0] for a in kept)

    def kernel(*refs):
        total, coarse = refs[-2:]
        s = whole(refs[:n]) + whole(refs[n:-2])
        total[...] = s
        coarse[...] = s.astype(bf16)

    return call(
        kernel, [((rows, cols), f32), ((rows, cols), bf16)], [VMEM] * (n + len(pieces)), name
    )(*kept, *pieces)


def hidden_units(mine, other, scale, pieces, name):
    rows, cols = mine.shape
    n, step = cols // 2, rows // pieces

    def kernel(mine, other, *outs):
        gate = (mine[:, :n] + other[:, :n].astype(f32)) * scale
        up = (mine[:, n:] + other[:, n:].astype(f32)) * scale
        hidden = (jax.nn.silu(gate) * up).astype(bf16)
        for i, out in enumerate(outs):
            out[...] = hidden[i * step : (i + 1) * step]

    return list(call(kernel, [((step, n), bf16)] * pieces, [VMEM, VMEM], name)(mine, other))


def down(where, steps, own, per, mine, others, wd, left, dtype, pieces, name):
    n, rows = len(mine), sum(m.shape[0] for m in mine)
    cols = wd.shape[1]
    each, count = rows // len(steps), pieces * len(steps)
    tile, step = 4 * LANES, rows // count

    def kernel(where, *refs):
        hm, ho, (wd, left), outs = refs[:n], refs[n : 2 * n], refs[2 * n : 2 * n + 2], refs[2 * n + 2 :]
        both = jnp.concatenate([whole(hm), whole(ho)], 0)
        pick = jnp.concatenate(
            [
                members_of(where, d, part, each, own * per // 2, own, per, left.shape[0])
                for part in (where[0], 1 - where[0])
                for d in steps
            ],
            0,
        )
        rows_left = jnp.dot(pick, left[...], preferred_element_type=f32)
        proj = jnp.sum(both.astype(f32) * rows_left, axis=1, keepdims=True)
        proj = jnp.broadcast_to(proj, (2 * rows, LANES))
        for t in range(0, cols + LANES, tile):
            at = slice(t, min(cols, t + tile)) if t < cols else slice(cols, cols + LANES)
            prod = jnp.dot(both, wd[:, at], preferred_element_type=f32) if t < cols else proj
            for i, out in enumerate(outs):
                out[:, at] = prod[i * step : (i + 1) * step].astype(dtype)

    outs = call(
        kernel,
        [((step, cols + LANES), dtype)] * (2 * count),
        [SMEM] + [VMEM] * (2 * n + 2),
        name,
    )(where, *mine, *others, wd, left)
    return list(outs[:count]), list(outs[count:])


def fold(base, got, pieces):
    rows, cols = got[0].shape
    half, step = rows // 2, rows // 2 // pieces
    n = len(base)

    def kernel(*refs):
        base_refs, got_refs, outs = refs[:n], refs[n : n + len(got)], refs[n + len(got) :]
        each = rows // n
        for c in range(pieces):
            for q in range(2):
                at = q * half + c * step
                b = base_refs[at // each]
                s = b[at % each : at % each + step, :].astype(f32)
                for g in got_refs:
                    s += g[at : at + step, :].astype(f32)
                outs[c][q * step : (q + 1) * step, :] = s.astype(outs[c].dtype)

    return call(
        kernel,
        [((2 * step, cols), bf16 if c else f32) for c in range(pieces)],
        [VMEM] * (n + len(got)),
        "fold",
    )(*base, *got)


def finish(where, mine, theirs, down_right, scale):
    half, deep = mine.shape[0], down_right.shape[1]
    rows, own = 2 * half, down_right.shape[0]

    def kernel(where, mine, theirs, right, out):
        first = where[0] == 0
        a = jnp.where(first, mine[...], theirs[...])
        b = jnp.where(first, theirs[...], mine[...])
        total = jnp.concatenate([a, b], 0)
        r = lax.broadcasted_iota(jnp.int32, (rows, own), 0) // (rows // own)
        pick = (r == lax.broadcasted_iota(jnp.int32, (rows, own), 1)).astype(bf16)
        right_rows = jnp.dot(pick, right[...], preferred_element_type=f32)
        shaped = total[:, :deep] + noise_scale * total[:, deep : deep + 1] * right_rows
        out[...] = (shaped * scale).astype(out.dtype)

    return call(
        kernel,
        [((rows, deep), bf16)],
        [SMEM] + [VMEM] * 3,
        "finish",
        out_specs=(VMEM,),
    )(where, mine, theirs, down_right)[0]


def update(where, own, factors, start, right, weight, step_coef, transposed=False):
    rows, cols = weight.shape
    members, n = right.shape[0], len(factors)
    parts = 4 if rows % (4 * LANES) == 0 else max(1, rows // LANES)
    step = rows // parts

    def kernel(where, *refs):
        pieces, (r, w, out, buf, sem) = refs[:n], refs[n:]
        order = gathered_order(where, own, members)
        moved = jnp.dot(order, r[...], preferred_element_type=f32).astype(bf16)
        copies = []
        for i in range(parts):
            at = slice(i * step, (i + 1) * step)
            take = slice(start, start + cols) if transposed else slice(start + i * step, start + (i + 1) * step)
            side = jnp.concatenate([p[:, take] for p in pieces], 0)
            left, other = (moved[:, at], side) if transposed else (side, moved)
            term = lax.dot_general(
                left, other, (((0,), (0,)), ((), ())), preferred_element_type=f32
            )
            buf[at, :] = (w[at, :].astype(f32) + step_coef * term).astype(bf16)
            here = pl.ds(i * step, step)
            copies.append(pltpu.make_async_copy(buf.at[here], out.at[here], sem.at[i]))
            copies[-1].start()
        for c in copies:
            c.wait()

    return call(
        kernel,
        [((rows, cols), weight.dtype)],
        [SMEM] + [VMEM] * (n + 2),
        "update",
        [pltpu.VMEM((rows, cols), bf16), pltpu.SemaphoreType.DMA((parts,))],
        out_specs=(ANY,),
    )(where, *factors, right, weight)[0]


def on_device(
    tokens,
    gate_weight,
    up_weight,
    down_weight,
    gate_left,
    gate_right,
    up_left,
    up_right,
    down_left,
    down_right,
    fitness,
):
    rows, deep = tokens.shape
    own = gate_left.shape[0]
    members = fitness.shape[0]
    per = rows // own
    d_model = deep * lax.axis_size("narrow")
    d_hidden = gate_weight.shape[1] * lax.axis_size("wide")
    w = lax.axis_index("wide")
    where = jnp.stack(
        [lax.axis_index("narrow") % 2, w // (NH * NZ), (w // NZ) % NH, w % NZ]
    ).astype(jnp.int32)

    packed, weighted = prepare(where, fitness, tokens, gate_left, up_left, down_right)

    over = from_h(packed, "tokens_xhi")
    weighted_over = from_h(weighted, "factors_xhi")
    gate_weight, up_weight = resident(after(gate_weight, packed), up_weight)
    mine, theirs = split_halves(where, after(packed, gate_weight), over)
    block = stack([mine] + from_core([theirs], "tokens_core"))
    parts = [block] + [early(block, d, f"tokens_early{d}") for d in STEPS[1:]]
    (down_weight,) = resident(after(down_weight, block))
    line = stack([after(block, down_weight, weighted_over)] + parts[1:], 2)
    lines = {0: line, **{d: late(line, d, f"tokens_late{d}") for d in STEPS[1:3]}}
    n = line.shape[0] // 2

    def exchange(d, x):
        return from_core(cut(x, n, 4), f"rows_core{d}")

    def project(d, x, others, count=4):
        return gate_up(count, where, d, own, per, x, others, gate_weight, up_weight, gate_right, up_right)

    def activate(mine, other, pieces, name):
        return hidden_units(mine, other, d_model**-0.5, pieces, name)

    def contract(steps, hidden, others, dtype, pieces, name):
        kept, sent = down(
            where, steps, own, per, hidden, others, down_weight, down_left, dtype, pieces, name
        )
        return kept, from_core(sent, f"{name}_core")

    keep0, send0 = project(0, line, exchange(0, line))
    mine0, coarse0 = add_both([keep0], from_core(send0, "sums_core0"), "add0")
    lines[2] = late(after(lines[1], coarse0), 1, "tokens_late2")
    x = after(lines[1], coarse0)
    others1, others3 = exchange(1, x), exchange(3, after(lines[3], coarse0))
    keep1, send1 = project(1, x, after(others1, others3), 2)
    keep3, send3 = project(3, after(lines[3], keep1), others3)
    got1 = from_core(send1, "sums_core1")
    mine13, coarse13 = add_both(
        [keep1, keep3], got1 + from_core(send3, "sums_core3"), "add13"
    )
    other13 = from_x(coarse13, "sums_x13")

    x = after(lines[2], coarse13)
    others2 = exchange(2, x)

    weighted = after(jnp.concatenate([weighted, weighted_over], 0), others2)
    factor_line = stack([weighted] + [early(weighted, d, f"factors_early{d}") for d in STEPS[1:]])

    keep2, send2 = project(2, x, others2)
    mine2, coarse2 = add_both([keep2], from_core(send2, "sums_core2"), "add2")
    other2 = from_x(coarse2, "sums_x2")
    factors = {0: factor_line, **{d: late(factor_line, d, f"factors_late{d}") for d in STEPS[1:]}}

    hidden13 = activate(after(mine13, coarse2), other13, 2, "hidden13")
    hidden13_o = from_core(hidden13, "hidden_core13")
    kept, sent = contract([1, 3], hidden13, hidden13_o, bf16, 2, "down13")
    kept = after(kept, other2, factors[1], factors[3])
    out1, out3 = stack(kept[:2] + sent[:2]), stack(kept[2:] + sent[2:])
    sum1, sum3 = late(out1, 3, "out_late1"), late(out3, 1, "out_late3")


    hidden2 = activate(after(mine2, out1, out3), other2, 2, "hidden2")
    kept, sent = contract([2], hidden2, from_core(hidden2, "hidden_core2"), bf16, 4, "down2")
    out2 = stack(after(kept, factors[2]) + sent)
    sum2 = late(out2, 2, "out_late2")

    other0 = from_x(after(coarse0, out2), "sums_x0")
    hidden0 = activate(after(mine0, out2), other0, 4, "hidden0")
    hidden0_o = from_core(hidden0, "hidden_core0")
    kept0, sent0 = down(
        where, [0], own, per, hidden0, hidden0_o, down_weight, down_left, f32, 2, "down0"
    )
    sent0 = from_core(after(sent0, sum1, sum3), "down0_core")

    pieces = fold(kept0 + sent0, [sum1, sum3, sum2], len(STEPS))
    got = [early(p, 4 - d, f"out_early{d}") for p, d in zip(pieces[1:], STEPS[1:])]

    step_coef = step_size / math.sqrt(members)
    factors = after([factors[d] for d in STEPS], pieces[0])
    new_gate = update(where, own, factors, 0, gate_right, gate_weight, step_coef)
    new_up = update(where, own, factors, deep, up_right, up_weight, step_coef)
    ours, away = fold([after(pieces[0], new_gate, new_up)], got, NH)
    factors = after(factors, ours)
    new_down = update(
        where, own, factors, 2 * deep, down_left, down_weight, step_coef, True
    )
    both = fold([after(ours, new_down)], [from_h(away, "out_xhi")], 1)[0]
    half = rows // 2
    (theirs,) = from_core([both[half:]], "out_core")
    mlp_out = finish(where, both[:half], theirs, down_right, d_hidden**-0.5)
    return (mlp_out, new_gate, new_up, new_down)


def solution(mesh):
    placed = (
        P("wide", "narrow"),
        P("narrow", "wide"),
        P("narrow", "wide"),
        P("wide", "narrow"),
        P("wide", "narrow"),
        P(None, "wide"),
        P("wide", "narrow"),
        P(None, "wide"),
        P(None, "wide"),
        P("wide", "narrow"),
        P(),
    )
    return jax.shard_map(
        on_device,
        mesh=mesh,
        in_specs=placed,
        out_specs=(
            P("wide", "narrow"),
            P("narrow", "wide"),
            P("narrow", "wide"),
            P("wide", "narrow"),
        ),
        check_vma=False,
    )
```
